32 devices in a mesh: expert: 8 (over y, x, core), dp: 4 (over z).
Axes of the slice: x: 2, y: 2, z: 4, core: 2. Of those that a mesh axis runs over, the one named last changes fastest.
Arguments:
- tokens: bfloat16 [4096, 2048], P(('expert', 'dp')), may hold values from -6 to 6
- routes: int32 [4096, 2], P(('expert', 'dp')), may hold values from 0 to 31, all different within a row; in each aligned block of 128 rows (0 to 127, 128 to 255, ...) at most 16 rows name the same one
- gate_probs: float32 [4096, 2], P(('expert', 'dp')), may hold values from 0.05 to 1
- norm_gain: float32 [2048], replicated, may hold values from 0.1 to 1.9
- w_gate: bfloat16 [32, 2048, 768], P(('expert', 'dp')), may hold values from -0.125 to 0.125
- w_up: bfloat16 [32, 2048, 768], P(('expert', 'dp')), may hold values from -0.125 to 0.125
- w_down: bfloat16 [32, 768, 2048], P(('expert', 'dp')), may hold values from -0.21875 to 0.21875
- out_grad: bfloat16 [4096, 2048], P(('expert', 'dp')), may hold values from -6 to 6
Outputs:
- mixed: bfloat16 [4096, 2048], P(('expert', 'dp'))
- grad_probs: float32 [4096, 2], P(('expert', 'dp'))
- grad_gain: float32 [2048], replicated
- grad_tokens: bfloat16 [4096, 2048], P(('expert', 'dp'))
- grad_gate: bfloat16 [32, 2048, 768], P(('expert', 'dp'))
- grad_up: bfloat16 [32, 2048, 768], P(('expert', 'dp'))
- grad_down: bfloat16 [32, 768, 2048], P(('expert', 'dp'))
The draws below stay inside these ranges and needn't reach their ends.
Inputs may be any that keep to these rules, and one draw needn't show every extreme that they name: `routes`: each row names 2 different experts. Among the 128 rows of one device no expert is named more than 16 times, a bound that some block reaches.
All inputs are finite; a program needn't handle non-finite values.
Results may differ from the reference program's by a relative error of at most 0.0072.
Values may be sent and summed in bfloat16 or wider, within the bound.
A program may use at most 128 MiB of HBM per device.

```python
import math
import jax
import jax.numpy as jnp
import numpy as np
from jax import lax

D = 2048
FF = 768
TOP = 2
TOK_DEV = 128
EXPERTS = 32
TOKENS = 4096
MOST = 16


def levels(own_key, extent, pieces, least, high):
    loudness, own = 1.0, jax.random.fold_in(own_key, 6)
    for position, blocks in pieces:
        draws = jnp.exp(jax.random.uniform(jax.random.fold_in(own, position), (blocks,), jnp.float32, least / len(pieces), high / len(pieces)))
        loudness = loudness * jnp.repeat(draws, extent[position] // blocks).reshape([-1 if axis == position else 1 for axis in range(len(extent))])
    return loudness


def routed_block(rng, own, number, rows, number_of, top, limit, skew):
    ranking = jax.random.permutation(rng, number_of)
    heavy_load, common = shares(number_of, rows * top, limit, skew, True), shares(number_of, rows * top, limit, skew, False)
    places = jnp.arange(number_of)

    def named(lengths, offset_by):
        used = int((lengths > 0).sum())
        fixed = max(1, used // 4)
        moved = fixed + (places - fixed + offset_by * (used - fixed)) % max(1, number_of - fixed)
        return jnp.zeros((number_of,), jnp.int32).at[ranking[jnp.where(places < fixed, places, moved)]].set(jnp.asarray(lengths, jnp.int32))

    lengths = jnp.where(number % 4 == 0, named(heavy_load, number // 4), named(common, number - number // 4 - 1))
    mixed = jax.random.permutation(jax.random.fold_in(own, 3), number_of)
    donor, sink = mixed[0:number_of // 2 * 2:2], mixed[1:number_of // 2 * 2:2]
    slack = jnp.minimum(lengths[donor] - 1, limit - lengths[sink]) // 2
    slack = jnp.where((donor == ranking[0]) | (sink == ranking[0]) | (lengths[sink] == 0), 0, jnp.maximum(slack, 0))
    moved = jax.random.randint(jax.random.fold_in(own, 4), (number_of // 2,), 0, 1 << 20) % (slack + 1)
    lengths = lengths.at[donor].add(-moved).at[sink].add(moved)
    items = jnp.searchsorted(jnp.cumsum(lengths), jnp.arange(rows * top), side="right").astype(jnp.int32)
    listing = items.reshape(top, rows).T
    listing = listing[jax.random.permutation(jax.random.fold_in(own, 1), rows)]
    offset_by = jax.random.randint(jax.random.fold_in(own, 2), (rows, 1), 0, top)
    return jnp.take_along_axis(listing, (jnp.arange(top)[None, :] + offset_by) % top, axis=1)


def shares(count, total, bound, slope, full):
    portions = [(1 << 20) // math.isqrt(grade ** slope) + 1 for grade in range(1, count + 1)]
    largest = bound if full else min(bound, max(-(-total // count), total * portions[0] // sum(portions)))
    least = 1 if total - largest >= count - 1 else 0
    holding, spare = [largest] + [least] * (count - 1), total - largest - least * (count - 1)
    while spare > 0:
        free = [i for i in range(1, count) if holding[i] < largest] or [i for i in range(1, count) if holding[i] < bound]
        whole, budget = sum([portions[i] for i in free]), spare
        for i in free:
            more = min(bound - holding[i], max(1, budget * portions[i] // whole), spare)
            holding[i] = holding[i] + more
            spare = spare - more
    return np.array(holding)


def scatter_about(rng, shape, scale, bound, split=(), kind=jnp.bfloat16):
    factor_of = levels(rng, shape, split, -0.22, 0.18) if split else 1.0
    drawn = jax.random.normal(rng, shape, jnp.float32) * scale * factor_of
    return jnp.minimum(jnp.maximum(drawn, -bound), bound).astype(kind)


def setup_inputs(seed: int = 0) -> dict:
    seeds = jax.random.split(jax.random.key(seed), 9)
    tokens = scatter_about(seeds[0], (TOKENS, D), 1.0, 6.0, ((0, 32),))
    routes_keys = jax.random.split(jax.random.fold_in(seeds[1], 1), TOKENS // TOK_DEV)
    routes_turns = jax.random.permutation(jax.random.fold_in(seeds[1], 3), TOKENS // TOK_DEV)
    routes = jax.vmap(lambda own, number: routed_block(jax.random.fold_in(seeds[1], 2), own, number, TOK_DEV, EXPERTS, TOP, MOST, 4))(routes_keys, routes_turns).reshape((TOKENS, TOP))
    gate_probs = jnp.clip(jnp.exp(math.log(1.0) - 2.9957323 * jax.random.uniform(seeds[2], (TOKENS, TOP), jnp.float32) ** levels(seeds[2], (TOKENS, TOP), ((0, 32),), -0.2, 0.2)), 0.05, 1.0)
    norm_gain = jnp.clip(1.0 + 0.18 * jax.random.normal(seeds[3], (D,), jnp.float32), 0.1, 1.9)
    w_gate = scatter_about(seeds[4], (EXPERTS, D, FF), D ** -0.5, 0.125, ((0, 32),))
    w_up = scatter_about(seeds[5], (EXPERTS, D, FF), D ** -0.5, 0.125, ((0, 32),))
    w_down = scatter_about(seeds[6], (EXPERTS, FF, D), FF ** -0.5, 0.21875, ((0, 32),))
    out_grad = scatter_about(seeds[7], (TOKENS, D), 1.0, 6.0, ((0, 32),))
    return dict(tokens=tokens, routes=routes, gate_probs=gate_probs, norm_gain=norm_gain, w_gate=w_gate, w_up=w_up, w_down=w_down, out_grad=out_grad)


def slots_of(block_ids):
    onehot = (block_ids[:, None] == jnp.arange(EXPERTS, dtype=jnp.int32)[None, :]).astype(jnp.int32)
    earlier = jnp.cumsum(onehot, axis=0) - onehot
    return (block_ids * MOST + lax.optimization_barrier(jnp.sum(earlier * onehot, axis=1))).astype(jnp.int32)

def expert_pass(packed):
    arrived, arrived_grad, gate_matrix, up_matrix, down_matrix = packed
    pre_gate = jnp.dot(arrived, gate_matrix, preferred_element_type=jnp.float32)
    up_value = jnp.dot(arrived, up_matrix, preferred_element_type=jnp.float32)
    sigmoid_gate = jax.nn.sigmoid(pre_gate)
    activated = pre_gate * sigmoid_gate
    hidden = (activated * up_value).astype(jnp.bfloat16)
    expert_out = jnp.dot(hidden, down_matrix, preferred_element_type=jnp.float32).astype(jnp.bfloat16)
    grad_hidden = lax.dot_general(arrived_grad, down_matrix, (((1,), (1,)), ((), ())), preferred_element_type=jnp.float32)
    grad_down = lax.dot_general(hidden, arrived_grad, (((0,), (0,)), ((), ())), preferred_element_type=jnp.float32).astype(jnp.bfloat16)
    grad_pre = (grad_hidden * up_value * sigmoid_gate * (1.0 + pre_gate * (1.0 - sigmoid_gate))).astype(jnp.bfloat16)
    grad_upval = (grad_hidden * activated).astype(jnp.bfloat16)
    grad_back = (lax.dot_general(grad_pre, gate_matrix, (((1,), (1,)), ((), ())), preferred_element_type=jnp.float32) + lax.dot_general(grad_upval, up_matrix, (((1,), (1,)), ((), ())), preferred_element_type=jnp.float32)).astype(jnp.bfloat16)
    grad_gate = lax.dot_general(arrived, grad_pre, (((0,), (0,)), ((), ())), preferred_element_type=jnp.float32).astype(jnp.bfloat16)
    grad_up = lax.dot_general(arrived, grad_upval, (((0,), (0,)), ((), ())), preferred_element_type=jnp.float32).astype(jnp.bfloat16)
    return (expert_out, grad_back, grad_gate, grad_up, grad_down)

def place(slot_index, rows):
    return jnp.zeros((EXPERTS * MOST, D), rows.dtype).at[slot_index].set(rows)

def to_experts(buffers, blocks):
    return buffers.reshape(blocks, EXPERTS, MOST, D).transpose(1, 0, 2, 3).reshape(EXPERTS, blocks * MOST, D)

def from_experts(buffers, blocks):
    return buffers.reshape(EXPERTS, blocks, MOST, D).transpose(1, 0, 2, 3).reshape(blocks, EXPERTS * MOST, D)

def pick(buffer, slot_index):
    return buffer[slot_index]

def reference(tokens, routes, gate_probs, norm_gain, w_gate, w_up, w_down, out_grad):
    blocks = TOKENS // TOK_DEV
    assigned = TOK_DEV * TOP
    inputs = tokens.astype(jnp.float32)
    inverse_rms = lax.rsqrt(lax.optimization_barrier(jnp.mean(inputs * inputs, axis=1, keepdims=True)) + 1e-06)
    normed = inputs * inverse_rms
    scaled = (normed * norm_gain).astype(jnp.bfloat16)
    slots = jax.vmap(slots_of)(routes.reshape(blocks, assigned).astype(jnp.int32))
    rows = jnp.repeat(scaled, TOP, axis=0).reshape(blocks, assigned, D)
    sent = to_experts(jax.vmap(place)(slots, rows), blocks)
    grad_in = out_grad.astype(jnp.float32)
    weights = gate_probs[:, :, None]
    grad_rows = (weights * grad_in[:, None, :]).astype(jnp.bfloat16).reshape(blocks, assigned, D)
    sent_grad = to_experts(jax.vmap(place)(slots, grad_rows), blocks)
    expert_out, grad_back, grad_gate, grad_up, grad_down = lax.map(expert_pass, (sent, sent_grad, w_gate, w_up, w_down))
    picked = jax.vmap(pick)(from_experts(expert_out, blocks), slots).reshape(TOKENS, TOP, D).astype(jnp.float32)
    mixed = (inputs + lax.optimization_barrier(jnp.sum(weights * picked, axis=1))).astype(jnp.bfloat16)
    grad_probs = lax.optimization_barrier(jnp.sum(grad_in[:, None, :] * picked, axis=2))
    back = jax.vmap(pick)(from_experts(grad_back, blocks), slots).reshape(TOKENS, TOP, D).astype(jnp.float32)
    grad_normed = lax.optimization_barrier(jnp.sum(back, axis=1))
    grad_gain = lax.optimization_barrier(jnp.sum(grad_normed * normed, axis=0))
    grad_scaled = grad_normed * norm_gain
    grad_tokens = (grad_in + inverse_rms * (grad_scaled - normed * lax.optimization_barrier(jnp.mean(grad_scaled * normed, axis=1, keepdims=True)))).astype(jnp.bfloat16)
    return (mixed, grad_probs, grad_gain, grad_tokens, grad_gate, grad_up, grad_down)
```

```python
import jax
import jax.numpy as jnp
from jax import lax
from jax.sharding import PartitionSpec as P


def outward(rows, capacity):
    width = rows.shape[-1]
    shaped = rows.reshape(lax.axis_size(("expert", "dp")), capacity, width)
    moved = lax.all_to_all(shaped, ("expert", "dp"), split_axis=0, concat_axis=0, tiled=True)
    return moved.reshape(rows.shape)


def inward(rows, capacity):
    width = rows.shape[-1]
    shaped = rows.reshape(lax.axis_size(("expert", "dp")), capacity, width)
    moved = lax.all_to_all(shaped, ("expert", "dp"), split_axis=0, concat_axis=0, tiled=True)
    return moved.reshape(rows.shape)


def contract(left, right, left_dim, right_dim):
    return lax.dot_general(
        left, right, (((left_dim,), (right_dim,)), ((), ())), preferred_element_type=jnp.float32
    )


def forward_expert(arrived, gate_matrix, up_matrix, down_matrix):
    pre_gate = jnp.dot(arrived, gate_matrix, preferred_element_type=jnp.float32)
    up_value = jnp.dot(arrived, up_matrix, preferred_element_type=jnp.float32)
    sigmoid_gate = jax.nn.sigmoid(pre_gate)
    activated = pre_gate * sigmoid_gate
    hidden = (activated * up_value).astype(jnp.bfloat16)
    expert_out = jnp.dot(hidden, down_matrix, preferred_element_type=jnp.float32).astype(
        jnp.bfloat16
    )
    return (pre_gate, up_value, sigmoid_gate, activated, hidden, expert_out)


def backward_expert(arrived, arrived_grad, saved, gate_matrix, up_matrix, down_matrix):
    pre_gate, up_value, sigmoid_gate, activated, hidden = saved
    grad_hidden = contract(arrived_grad, down_matrix, 1, 1)
    grad_down = contract(hidden, arrived_grad, 0, 0).astype(jnp.bfloat16)
    grad_pre = (
        grad_hidden * up_value * sigmoid_gate * (1.0 + pre_gate * (1.0 - sigmoid_gate))
    ).astype(jnp.bfloat16)
    grad_upval = (grad_hidden * activated).astype(jnp.bfloat16)
    grad_back = (
        contract(grad_pre, gate_matrix, 1, 1) + contract(grad_upval, up_matrix, 1, 1)
    ).astype(jnp.bfloat16)
    grad_gate = contract(arrived, grad_pre, 0, 0).astype(jnp.bfloat16)
    grad_up = contract(arrived, grad_upval, 0, 0).astype(jnp.bfloat16)
    return (grad_back, grad_gate, grad_up, grad_down)


def on_device(tokens, routes, gate_probs, norm_gain, w_gate, w_up, w_down, out_grad):
    devices_all = lax.axis_size(("expert", "dp"))
    tok_rows, width = tokens.shape
    top_count = routes.shape[1]
    assigned = tok_rows * top_count
    capacity = 2 * assigned // devices_all
    inputs = tokens.astype(jnp.float32)
    inverse_rms = lax.rsqrt(jnp.mean(inputs * inputs, axis=1, keepdims=True) + 1e-06)
    normed = inputs * inverse_rms
    scaled = (normed * norm_gain).astype(jnp.bfloat16)
    flat_ids = routes.reshape(assigned)
    places = jnp.arange(assigned, dtype=jnp.int32)
    same = flat_ids[:, None] == flat_ids[None, :]
    before = places[None, :] < places[:, None]
    rank = jnp.sum((same & before).astype(jnp.int32), axis=1)
    slot_index = flat_ids * capacity + rank
    gate_matrix = w_gate[0]
    up_matrix = w_up[0]
    down_matrix = w_down[0]
    weights = gate_probs[:, :, None]
    grad_in = out_grad.astype(jnp.float32)
    grad_rows = (weights * grad_in[:, None, :]).astype(jnp.bfloat16).reshape(assigned, width)
    repeated = jnp.repeat(scaled, top_count, axis=0)
    empty = jnp.zeros((devices_all * capacity, width), jnp.bfloat16)
    arrived = outward(empty.at[slot_index].set(repeated), capacity)
    pre_gate, up_value, sigmoid_gate, activated, hidden, expert_out = forward_expert(
        arrived, gate_matrix, up_matrix, down_matrix
    )
    returned = inward(expert_out, capacity)
    picked = returned[slot_index].reshape(tok_rows, top_count, width).astype(jnp.float32)
    arrived_grad = outward(empty.at[slot_index].set(grad_rows), capacity)
    grad_back, grad_gate, grad_up, grad_down = backward_expert(
        arrived,
        arrived_grad,
        (pre_gate, up_value, sigmoid_gate, activated, hidden),
        gate_matrix,
        up_matrix,
        down_matrix,
    )
    returned_grad = inward(grad_back, capacity)
    grad_normed = jnp.sum(
        returned_grad[slot_index].reshape(tok_rows, top_count, width).astype(jnp.float32), axis=1
    )
    mixed = (inputs + jnp.sum(weights * picked, axis=1)).astype(jnp.bfloat16)
    grad_probs = jnp.sum(grad_in[:, None, :] * picked, axis=2)
    gain_part = jnp.sum(grad_normed * normed, axis=0)
    grad_gain = lax.psum(gain_part, ("expert", "dp"))
    grad_scaled = grad_normed * norm_gain
    grad_tokens = (
        grad_in
        + inverse_rms
        * (grad_scaled - normed * jnp.mean(grad_scaled * normed, axis=1, keepdims=True))
    ).astype(jnp.bfloat16)
    return (
        mixed,
        grad_probs,
        grad_gain,
        grad_tokens,
        grad_gate[None],
        grad_up[None],
        grad_down[None],
    )


def solution(mesh):
    return jax.shard_map(
        on_device,
        mesh=mesh,
        in_specs=(
            P(("expert", "dp"), None),
            P(("expert", "dp"), None),
            P(("expert", "dp"), None),
            P(),
            P(("expert", "dp"), None, None),
            P(("expert", "dp"), None, None),
            P(("expert", "dp"), None, None),
            P(("expert", "dp"), None),
        ),
        out_specs=(
            P(("expert", "dp"), None),
            P(("expert", "dp"), None),
            P(),
            P(("expert", "dp"), None),
            P(("expert", "dp"), None, None),
            P(("expert", "dp"), None, None),
            P(("expert", "dp"), None, None),
        ),
        check_vma=False,
    )
```

```python
import jax
import jax.numpy as jnp
from jax import lax
from jax.sharding import PartitionSpec as P

BOTH = ("expert", "dp")


def contract(left, right, left_dim, right_dim):
    return lax.dot_general(
        left, right, (((left_dim,), (right_dim,)), ((), ())), preferred_element_type=jnp.float32
    )


def exchange(rows):
    shaped = rows.reshape(lax.axis_size(BOTH), -1, rows.shape[-1])
    return lax.all_to_all(shaped, BOTH, split_axis=0, concat_axis=0, tiled=True).reshape(
        rows.shape
    )


def slots_of(routes, capacity):
    columns = [routes[:, k] for k in range(routes.shape[1])]
    places = jnp.arange(routes.shape[0], dtype=jnp.int32)
    earlier = places[None, :] < places[:, None]
    return [
        own * capacity
        + jnp.sum(
            sum(((own[:, None] == other[None, :]) & earlier).astype(jnp.int32) for other in columns),
            axis=1,
        )
        for own in columns
    ]


def on_device(tokens, routes, gate_probs, norm_gain, w_gate, w_up, w_down, out_grad):
    devices_all = lax.axis_size(BOTH)
    tok_rows, width = tokens.shape
    top_count = routes.shape[1]
    capacity = 2 * tok_rows * top_count // devices_all
    gate_matrix, up_matrix, down_matrix = w_gate[0], w_up[0], w_down[0]

    inputs = tokens.astype(jnp.float32)
    inverse_rms = lax.rsqrt(jnp.mean(inputs * inputs, axis=1, keepdims=True) + 1e-06)
    normed = inputs * inverse_rms
    scaled = (normed * norm_gain).astype(jnp.bfloat16)

    numbers = jnp.arange(devices_all * capacity, dtype=jnp.int32)[:, None]
    hits = [slot[None, :] == numbers for slot in slots_of(routes, capacity)]
    picks = [h.astype(jnp.bfloat16) for h in hits]
    chosen = sum(picks)
    slot_weight = sum(
        jnp.sum(jnp.where(h, gate_probs[None, :, k], 0.0), axis=1) for k, h in enumerate(hits)
    )[:, None]

    arrived = exchange(contract(chosen, scaled, 1, 0).astype(jnp.bfloat16))
    arrived_grad = exchange(
        (slot_weight * contract(chosen, out_grad, 1, 0)).astype(jnp.bfloat16)
    )

    pre_gate = contract(arrived, gate_matrix, 1, 0)
    up_value = contract(arrived, up_matrix, 1, 0)
    sigmoid_gate = jax.nn.sigmoid(pre_gate)
    activated = pre_gate * sigmoid_gate
    hidden = (activated * up_value).astype(jnp.bfloat16)
    expert_out = contract(hidden, down_matrix, 1, 0).astype(jnp.bfloat16)
    expert_out, arrived_grad = lax.optimization_barrier((expert_out, arrived_grad))
    returned = exchange(expert_out)

    grad_hidden = contract(arrived_grad, down_matrix, 1, 1)
    grad_pre = (
        grad_hidden * up_value * sigmoid_gate * (1.0 + pre_gate * (1.0 - sigmoid_gate))
    ).astype(jnp.bfloat16)
    grad_upval = (grad_hidden * activated).astype(jnp.bfloat16)
    grad_back = (
        contract(grad_pre, gate_matrix, 1, 1) + contract(grad_upval, up_matrix, 1, 1)
    ).astype(jnp.bfloat16)
    returned, grad_back = lax.optimization_barrier((returned, grad_back))
    returned_grad = exchange(grad_back)
    grad_down = contract(hidden, arrived_grad, 0, 0).astype(jnp.bfloat16)
    grad_gate = contract(arrived, grad_pre, 0, 0).astype(jnp.bfloat16)
    grad_up = contract(arrived, grad_upval, 0, 0).astype(jnp.bfloat16)

    grad_in = out_grad.astype(jnp.float32)
    picked = [contract(pick, returned, 0, 0) for pick in picks]
    mixed = (inputs + sum(gate_probs[:, k : k + 1] * p for k, p in enumerate(picked))).astype(
        jnp.bfloat16
    )
    grad_probs = jnp.stack([jnp.sum(grad_in * p, axis=1) for p in picked], axis=1)

    grad_normed = contract(chosen, returned_grad, 0, 0)
    gain_part = jnp.sum(grad_normed * normed, axis=0)
    parts = exchange(jnp.broadcast_to(gain_part[None, :], (devices_all, width)))
    grad_gain = jnp.sum(parts, axis=0)
    grad_scaled = grad_normed * norm_gain
    grad_tokens = (
        grad_in
        + inverse_rms
        * (grad_scaled - normed * jnp.mean(grad_scaled * normed, axis=1, keepdims=True))
    ).astype(jnp.bfloat16)
    return (
        mixed,
        grad_probs,
        grad_gain,
        grad_tokens,
        grad_gate[None],
        grad_up[None],
        grad_down[None],
    )


def solution(mesh):
    rows, copied, blocks = P(BOTH, None), P(), P(BOTH, None, None)
    return jax.shard_map(
        on_device,
        mesh=mesh,
        in_specs=(rows, rows, rows, copied, blocks, blocks, blocks, rows),
        out_specs=(rows, rows, copied, rows, blocks, blocks, blocks),
        check_vma=False,
    )
```

```python
import jax
import jax.numpy as jnp
from jax import lax
from jax.experimental import pallas as pl
from jax.experimental.pallas import tpu as pltpu
from jax.sharding import PartitionSpec as P

BOTH = ("expert", "dp")


def contract(left, right, left_dim, right_dim):
    return lax.dot_general(
        left, right, (((left_dim,), (right_dim,)), ((), ())), preferred_element_type=jnp.float32
    )


def exchange(rows):
    shaped = rows.reshape(lax.axis_size(BOTH), -1, rows.shape[-1])
    return lax.all_to_all(shaped, BOTH, split_axis=0, concat_axis=0, tiled=True).reshape(
        rows.shape
    )


def slots_of(routes, capacity):
    columns = [routes[:, k] for k in range(routes.shape[1])]
    places = jnp.arange(routes.shape[0], dtype=jnp.int32)
    earlier = places[None, :] < places[:, None]
    return [
        own * capacity
        + jnp.sum(
            sum(((own[:, None] == other[None, :]) & earlier).astype(jnp.int32) for other in columns),
            axis=1,
        )
        for own in columns
    ]


def total_over_devices(part):
    for axis in reversed(BOTH):
        size, apart = lax.axis_size(axis), 1
        while apart < size:
            part = part + lax.ppermute(part, axis, [(i, i ^ apart) for i in range(size)])
            apart *= 2
    return part


def tokens_gradient_kernel(chosen_ref, back_ref, tokens_ref, gain_ref, grad_ref, out_ref):
    inputs = tokens_ref[...].astype(jnp.float32)
    inverse_rms = lax.rsqrt(jnp.mean(inputs * inputs, axis=1, keepdims=True) + 1e-06)
    normed = inputs * inverse_rms
    grad_normed = contract(chosen_ref[...], back_ref[...], 1, 0)
    grad_scaled = grad_normed * gain_ref[...]
    mean = jnp.mean(grad_scaled * normed, axis=1, keepdims=True)
    out_ref[...] = (
        grad_ref[...].astype(jnp.float32) + inverse_rms * (grad_scaled - normed * mean)
    ).astype(jnp.bfloat16)


def tokens_gradient(chosen, returned_grad, tokens, norm_gain, out_grad):
    rows, width = tokens.shape
    slots = chosen.shape[0]
    step = min(64, rows)
    own = pl.BlockSpec((step, width), lambda i: (i, 0))
    return pl.pallas_call(
        tokens_gradient_kernel,
        grid=(rows // step,),
        out_shape=jax.ShapeDtypeStruct((rows, width), jnp.bfloat16),
        in_specs=[
            pl.BlockSpec((step, slots), lambda i: (i, 0)),
            pl.BlockSpec((slots, width), lambda i: (0, 0)),
            own,
            pl.BlockSpec((1, width), lambda i: (0, 0)),
            own,
        ],
        out_specs=own,
        compiler_params=pltpu.CompilerParams(vmem_limit_bytes=24 * 2**20),
        cost_estimate=pl.CostEstimate(
            flops=2 * rows * slots * width,
            bytes_accessed=2 * width * (slots + 3 * rows),
            transcendentals=0,
        ),
    )(chosen.T, returned_grad, tokens, norm_gain[None, :], out_grad)


def on_device(tokens, routes, gate_probs, norm_gain, w_gate, w_up, w_down, out_grad):
    devices_all = lax.axis_size(BOTH)
    tok_rows, width = tokens.shape
    top_count = routes.shape[1]
    capacity = 2 * tok_rows * top_count // devices_all
    gate_matrix, up_matrix, down_matrix = w_gate[0], w_up[0], w_down[0]

    inputs = tokens.astype(jnp.float32)
    inverse_rms = lax.rsqrt(jnp.mean(inputs * inputs, axis=1, keepdims=True) + 1e-06)
    normed = inputs * inverse_rms
    scaled = (normed * norm_gain).astype(jnp.bfloat16)

    numbers = jnp.arange(devices_all * capacity, dtype=jnp.int32)[:, None]
    hits = [slot[None, :] == numbers for slot in slots_of(routes, capacity)]
    picks = [h.astype(jnp.bfloat16) for h in hits]
    chosen = sum(picks)
    slot_weight = sum(
        jnp.sum(jnp.where(h, gate_probs[None, :, k], 0.0), axis=1) for k, h in enumerate(hits)
    )[:, None]

    arrived = exchange(contract(chosen, scaled, 1, 0).astype(jnp.bfloat16))
    arrived_grad = exchange(
        (slot_weight * contract(chosen, out_grad, 1, 0)).astype(jnp.bfloat16)
    )

    pre_gate = contract(arrived, gate_matrix, 1, 0)
    up_value = contract(arrived, up_matrix, 1, 0)
    sigmoid_gate = jax.nn.sigmoid(pre_gate)
    activated = pre_gate * sigmoid_gate
    hidden = (activated * up_value).astype(jnp.bfloat16)
    expert_out = contract(hidden, down_matrix, 1, 0).astype(jnp.bfloat16)
    expert_out, arrived_grad = lax.optimization_barrier((expert_out, arrived_grad))
    returned = exchange(expert_out)

    grad_hidden = contract(arrived_grad, down_matrix, 1, 1)
    grad_pre = (
        grad_hidden * up_value * sigmoid_gate * (1.0 + pre_gate * (1.0 - sigmoid_gate))
    ).astype(jnp.bfloat16)
    grad_upval = (grad_hidden * activated).astype(jnp.bfloat16)
    grad_back = (
        contract(grad_pre, gate_matrix, 1, 1) + contract(grad_upval, up_matrix, 1, 1)
    ).astype(jnp.bfloat16)
    returned, grad_back = lax.optimization_barrier((returned, grad_back))
    returned_grad = exchange(grad_back)
    gain_part = jnp.sum(grad_back.astype(jnp.float32) * arrived.astype(jnp.float32), axis=0)
    grad_gain = total_over_devices(gain_part) / norm_gain
    grad_down = contract(hidden, arrived_grad, 0, 0).astype(jnp.bfloat16)
    grad_gate = contract(arrived, grad_pre, 0, 0).astype(jnp.bfloat16)
    grad_up = contract(arrived, grad_upval, 0, 0).astype(jnp.bfloat16)

    grad_in = out_grad.astype(jnp.float32)
    picked = [contract(pick, returned, 0, 0) for pick in picks]
    mixed = (inputs + sum(gate_probs[:, k : k + 1] * p for k, p in enumerate(picked))).astype(
        jnp.bfloat16
    )
    grad_probs = jnp.stack([jnp.sum(grad_in * p, axis=1) for p in picked], axis=1)

    grad_tokens = tokens_gradient(chosen, returned_grad, tokens, norm_gain, out_grad)
    return (
        mixed,
        grad_probs,
        grad_gain,
        grad_tokens,
        grad_gate[None],
        grad_up[None],
        grad_down[None],
    )


def solution(mesh):
    rows, copied, blocks = P(BOTH, None), P(), P(BOTH, None, None)
    return jax.shard_map(
        on_device,
        mesh=mesh,
        in_specs=(rows, rows, rows, copied, blocks, blocks, blocks, rows),
        out_specs=(rows, rows, copied, rows, blocks, blocks, blocks),
        check_vma=False,
    )
```

```python
import jax
import jax.numpy as jnp
from jax import lax
from jax.experimental import pallas as pl
from jax.experimental.pallas import tpu as pltpu
from jax.sharding import PartitionSpec as P

BOTH = ("expert", "dp")


def contract(left, right, left_dim, right_dim):
    return lax.dot_general(
        left, right, (((left_dim,), (right_dim,)), ((), ())), preferred_element_type=jnp.float32
    )


def exchange(rows):
    shaped = rows.reshape(lax.axis_size(BOTH), -1, rows.shape[-1])
    return lax.all_to_all(shaped, BOTH, split_axis=0, concat_axis=0, tiled=True).reshape(
        rows.shape
    )


def slots_of(routes, capacity):
    columns = [routes[:, k] for k in range(routes.shape[1])]
    places = jnp.arange(routes.shape[0], dtype=jnp.int32)
    earlier = places[None, :] < places[:, None]
    return [
        own * capacity
        + jnp.sum(
            sum(((own[:, None] == other[None, :]) & earlier).astype(jnp.int32) for other in columns),
            axis=1,
        )
        for own in columns
    ]


def total_over(part, axis):
    size, apart = lax.axis_size(axis), 1
    while apart < size:
        part = part + lax.ppermute(part, axis, [(i, i ^ apart) for i in range(size)])
        apart *= 2
    return part


def tokens_gradient_kernel(chosen_ref, back_ref, tokens_ref, gain_ref, grad_ref, out_ref):
    inputs = tokens_ref[...].astype(jnp.float32)
    inverse_rms = lax.rsqrt(jnp.mean(inputs * inputs, axis=1, keepdims=True) + 1e-06)
    normed = inputs * inverse_rms
    grad_normed = contract(chosen_ref[...], back_ref[...], 1, 0)
    grad_scaled = grad_normed * gain_ref[...]
    mean = jnp.mean(grad_scaled * normed, axis=1, keepdims=True)
    out_ref[...] = (
        grad_ref[...].astype(jnp.float32) + inverse_rms * (grad_scaled - normed * mean)
    ).astype(jnp.bfloat16)


def tokens_gradient(chosen, returned_grad, tokens, norm_gain, out_grad):
    rows, width = tokens.shape
    slots = chosen.shape[0]
    step = min(64, rows)
    own = pl.BlockSpec((step, width), lambda i: (i, 0))
    return pl.pallas_call(
        tokens_gradient_kernel,
        grid=(rows // step,),
        out_shape=jax.ShapeDtypeStruct((rows, width), jnp.bfloat16),
        in_specs=[
            pl.BlockSpec((step, slots), lambda i: (i, 0)),
            pl.BlockSpec((slots, width), lambda i: (0, 0)),
            own,
            pl.BlockSpec((1, width), lambda i: (0, 0)),
            own,
        ],
        out_specs=own,
        compiler_params=pltpu.CompilerParams(vmem_limit_bytes=56 * 2**20),
        cost_estimate=pl.CostEstimate(
            flops=2 * rows * slots * width,
            bytes_accessed=2 * width * (slots + 3 * rows),
            transcendentals=0,
        ),
    )(chosen.T, returned_grad, tokens, norm_gain[None, :], out_grad)


def on_device(tokens, routes, gate_probs, norm_gain, w_gate, w_up, w_down, out_grad):
    devices_all = lax.axis_size(BOTH)
    tok_rows, width = tokens.shape
    top_count = routes.shape[1]
    capacity = 2 * tok_rows * top_count // devices_all
    gate_matrix, up_matrix, down_matrix = w_gate[0], w_up[0], w_down[0]

    inputs = tokens.astype(jnp.float32)
    inverse_rms = lax.rsqrt(jnp.mean(inputs * inputs, axis=1, keepdims=True) + 1e-06)
    normed = inputs * inverse_rms
    scaled = (normed * norm_gain).astype(jnp.bfloat16)

    numbers = jnp.arange(devices_all * capacity, dtype=jnp.int32)[:, None]
    hits = [slot[None, :] == numbers for slot in slots_of(routes, capacity)]
    picks = [h.astype(jnp.bfloat16) for h in hits]
    chosen = sum(picks)
    slot_weight = sum(
        jnp.sum(jnp.where(h, gate_probs[None, :, k], 0.0), axis=1) for k, h in enumerate(hits)
    )[:, None]

    arrived = exchange(contract(chosen, scaled, 1, 0).astype(jnp.bfloat16))
    arrived_grad = exchange(
        (slot_weight * contract(chosen, out_grad, 1, 0)).astype(jnp.bfloat16)
    )

    pre_gate = contract(arrived, gate_matrix, 1, 0)
    up_value = contract(arrived, up_matrix, 1, 0)
    sigmoid_gate = jax.nn.sigmoid(pre_gate)
    activated = pre_gate * sigmoid_gate
    hidden = (activated * up_value).astype(jnp.bfloat16)
    expert_out = contract(hidden, down_matrix, 1, 0).astype(jnp.bfloat16)
    expert_out, arrived_grad = lax.optimization_barrier((expert_out, arrived_grad))
    returned = exchange(expert_out)

    grad_hidden = contract(arrived_grad, down_matrix, 1, 1)
    grad_pre = (
        grad_hidden * up_value * sigmoid_gate * (1.0 + pre_gate * (1.0 - sigmoid_gate))
    ).astype(jnp.bfloat16)
    grad_upval = (grad_hidden * activated).astype(jnp.bfloat16)
    grad_back = (
        contract(grad_pre, gate_matrix, 1, 1) + contract(grad_upval, up_matrix, 1, 1)
    ).astype(jnp.bfloat16)
    gain_part = jnp.sum(grad_back.astype(jnp.float32) * arrived.astype(jnp.float32), axis=0)
    gain_part = total_over(gain_part, "expert")
    returned, grad_back, gain_part = lax.optimization_barrier((returned, grad_back, gain_part))
    returned_grad = exchange(grad_back)
    grad_gain = total_over(gain_part, "dp") / norm_gain
    grad_down = contract(hidden, arrived_grad, 0, 0).astype(jnp.bfloat16)
    grad_gate = contract(arrived, grad_pre, 0, 0).astype(jnp.bfloat16)
    grad_up = contract(arrived, grad_upval, 0, 0).astype(jnp.bfloat16)

    grad_in = out_grad.astype(jnp.float32)
    picked = [contract(pick, returned, 0, 0) for pick in picks]
    mixed = (inputs + sum(gate_probs[:, k : k + 1] * p for k, p in enumerate(picked))).astype(
        jnp.bfloat16
    )
    grad_probs = jnp.stack([jnp.sum(grad_in * p, axis=1) for p in picked], axis=1)

    grad_tokens = tokens_gradient(chosen, returned_grad, tokens, norm_gain, out_grad)
    return (
        mixed,
        grad_probs,
        grad_gain,
        grad_tokens,
        grad_gate[None],
        grad_up[None],
        grad_down[None],
    )


def solution(mesh):
    rows, copied, blocks = P(BOTH, None), P(), P(BOTH, None, None)
    return jax.shard_map(
        on_device,
        mesh=mesh,
        in_specs=(rows, rows, rows, copied, blocks, blocks, blocks, rows),
        out_specs=(rows, rows, copied, rows, blocks, blocks, blocks),
        check_vma=False,
    )
```
